256 devices in a mesh: clip: 4 (over x), task: 64 (over y, z, core).
Axes of the slice: x: 4, y: 4, z: 8, core: 2. Of those that a mesh axis runs over, the one named last changes fastest.
Arguments:
- latents: bfloat16 [4, 256, 96, 384], P('clip', 'task'), may hold values from -6 to 6
- caches: bfloat16 [4, 64, 3, 2, 96, 384], P('clip', 'task'), may hold values from -6 to 6
- reward_grad: bfloat16 [4, 256, 96, 384], P('clip', 'task'), may hold values from -6 to 6
- weights: bfloat16 [3, 3, 384, 384], replicated, may hold values from -0.1875 to 0.1875
- biases: float32 [3, 384], replicated, may hold values from -3 to 3
- selected: int32 [4, 32], P('clip'), may hold values from 0 to 63, as said below
- destination: int32 [4, 64], P('clip', 'task'), may hold values from 0 to 3
Outputs:
- latent_grad: bfloat16 [4, 256, 96, 384], P('clip', 'task')
- replica_wgrad: float32 [4, 3456, 384], P('clip', 'task')
The draws below stay inside these ranges and needn't reach their ends.
Inputs may be any that keep to these rules, and one draw needn't show every extreme that they name: The entries of each row of selected are distinct.
All inputs are finite; a program needn't handle non-finite values.
Results may differ from the reference program's by a relative error of at most 0.0065.
Values may be sent and summed in bfloat16 or wider, within the bound.
A program may use at most 128 MiB of HBM per device.

```python
import jax
import jax.numpy as jnp
from jax import lax

CH = 384
FRAMES = 4
TAPS = 3
LAYERS = 3
SPOTS = 96
CLIPS = 4
POSITIONS = 64
PICKS = 32


def draw_selected(key, part):
    key = jax.random.fold_in(key, 5)
    keys = jax.random.split(key, CLIPS)
    picks = jax.vmap(lambda one: jax.random.permutation(one, POSITIONS)[:PICKS])(keys)
    return picks.astype(jnp.int32)


def touch_ends(drawn, key, smallest, largest):
    place = [jax.random.randint(jax.random.fold_in(key, axis), (), 0, length) for axis, length in enumerate(drawn.shape)]
    main_axis = drawn.shape.index(max(drawn.shape))
    beside = place[:main_axis] + [(place[main_axis] + 1) % drawn.shape[main_axis]] + place[main_axis + 1:]
    return drawn.at[tuple(place)].set(smallest).at[tuple(beside)].set(largest)


def block_levels(stream_key, shape, cuts, low, largest):
    def one(dim, parts):
        heights = jax.random.uniform(jax.random.fold_in(jax.random.fold_in(stream_key, 6), dim), (parts,), jnp.float32, low / len(cuts), largest / len(cuts))
        return jnp.repeat(jnp.exp(heights), shape[dim] // parts).reshape((-1,) + (1,) * (len(shape) - dim - 1))

    loudness = one(*cuts[0])
    for cut in cuts[1:]:
        loudness = loudness * one(*cut)
    return loudness


def centred(stream_key, dims, spread, reach, pieces=(), kind=jnp.bfloat16):
    level = block_levels(stream_key, dims, pieces, -0.22, 0.18) if pieces else 1.0
    values = jax.random.normal(stream_key, dims, jnp.float32) * spread * level
    return jnp.minimum(jnp.maximum(values, -reach), reach).astype(kind)


def setup_inputs(seed: int = 0) -> dict:
    streams_of = jax.random.split(jax.random.key(seed), 8)
    return {
        "latents": centred(streams_of[0], (CLIPS, POSITIONS * FRAMES, SPOTS, CH), 1.0, 6.0, ((0, 4), (1, 64))),
        "caches": centred(streams_of[1], (CLIPS, POSITIONS, LAYERS, TAPS - 1, SPOTS, CH), 1.0, 6.0, ((0, 4), (1, 64))),
        "reward_grad": centred(streams_of[2], (CLIPS, POSITIONS * FRAMES, SPOTS, CH), 1.0, 6.0, ((0, 4), (1, 64))),
        "weights": centred(streams_of[3], (LAYERS, TAPS, CH, CH), (TAPS * CH) ** -0.5, 0.1875),
        "biases": centred(streams_of[4], (LAYERS, CH), 0.7, 3.0, (), jnp.float32),
        "selected": draw_selected(jax.random.fold_in(streams_of[7], 71), 0),
        "destination": touch_ends(jax.random.randint(streams_of[6], (CLIPS, POSITIONS), 0, CLIPS), jax.random.fold_in(streams_of[6], 1), 0, CLIPS - 1).astype(jnp.int32),
    }


def group_forward(cache, latent, weights, biases):
    rows = FRAMES * SPOTS
    hidden = latent
    extended = []
    preacts = []
    for layer in range(LAYERS):
        joined = jnp.concatenate([cache[layer], hidden], 0)
        total = jnp.zeros((rows, CH), jnp.float32) + biases[layer][None, :]
        for tap in range(TAPS):
            window = joined[tap:tap + FRAMES].reshape(rows, CH)
            total = total + jnp.dot(window, weights[layer, tap], preferred_element_type=jnp.float32)
        hidden = (hidden.astype(jnp.float32) + jax.nn.silu(total).reshape(FRAMES, SPOTS, CH)).astype(jnp.bfloat16)
        extended.append(joined)
        preacts.append(total)
    return extended, preacts


def group_backward(extended, preacts, weights, upstream, incoming):
    rows = FRAMES * SPOTS
    lead = (TAPS - 1) * SPOTS
    grad = upstream
    outgoing = [None] * LAYERS
    deltas = [None] * LAYERS
    for layer in range(LAYERS - 1, -1, -1):
        preact = preacts[layer]
        sigma = jax.nn.sigmoid(preact)
        delta = (grad * sigma * (1.0 + preact * (1.0 - sigma))).astype(jnp.bfloat16)
        ext_grad = jnp.zeros((rows + lead, CH), jnp.float32)
        for tap in range(TAPS):
            part = jnp.dot(delta, weights[layer, tap].T, preferred_element_type=jnp.float32)
            ext_grad = ext_grad.at[tap * SPOTS:tap * SPOTS + rows].add(part)
        outgoing[layer] = ext_grad[:lead].astype(jnp.bfloat16).reshape(TAPS - 1, SPOTS, CH)
        tail = jnp.concatenate([jnp.zeros((rows - lead, CH), jnp.float32), incoming[layer].reshape(lead, CH).astype(jnp.float32)], 0)
        grad = grad + ext_grad[lead:] + tail
        deltas[layer] = delta
    return grad.astype(jnp.bfloat16), jnp.stack(outgoing), deltas


def kernel_grads(extended, deltas):
    rows = FRAMES * SPOTS
    blocks = []
    for layer in range(LAYERS):
        for tap in range(TAPS):
            window = extended[layer][tap:tap + FRAMES].reshape(rows, CH)
            blocks.append(jnp.dot(window.T, deltas[layer], preferred_element_type=jnp.float32))
    return jnp.concatenate(blocks, 0)


def reference(latents, caches, reward_grad, weights, biases, selected, destination):
    rows = FRAMES * SPOTS
    inputs = latents.reshape(CLIPS, POSITIONS, FRAMES, SPOTS, CH)
    upper = reward_grad.reshape(CLIPS, POSITIONS, FRAMES, SPOTS, CH)
    where = jnp.arange(POSITIONS, dtype=jnp.int32)
    chosen = jnp.any(selected[:, None, :] == where[None, :, None], axis=2).astype(jnp.float32)
    replicas = jnp.arange(CLIPS, dtype=jnp.int32)

    def one_group(latent, cache, grad_in, flag, incoming):
        extended, preacts = group_forward(cache, latent, weights, biases)
        upstream = grad_in.reshape(rows, CH).astype(jnp.float32) * flag
        latent_grad, outgoing, deltas = group_backward(extended, preacts, weights, upstream, incoming)
        return latent_grad, outgoing, kernel_grads(extended, deltas)

    def step(carry, position):
        incoming, total = carry
        latent_grad, outgoing, grads = jax.vmap(one_group)(inputs[:, position], caches[:, position], upper[:, position], chosen[:, position], incoming)
        onehot = (destination[:, position][:, None] == replicas[None, :]).astype(jnp.float32)
        total = total + jnp.einsum('cr,cij->rij', onehot, grads, precision=lax.Precision.HIGHEST)
        return (outgoing, total), latent_grad

    start = (jnp.zeros((CLIPS, LAYERS, TAPS - 1, SPOTS, CH), jnp.bfloat16), jnp.zeros((CLIPS, LAYERS * TAPS * CH, CH), jnp.float32))
    order = jnp.arange(POSITIONS - 1, -1, -1, dtype=jnp.int32)
    (last, total), grads_rev = lax.scan(step, start, order)
    grads_fwd = jnp.flip(grads_rev, 0)
    latent_grad = jnp.transpose(grads_fwd, (1, 0, 2, 3)).reshape(CLIPS, POSITIONS * FRAMES, SPOTS, CH)
    return latent_grad, total
```

```python
import jax
import jax.numpy as jnp
from jax import lax
from jax.experimental import pallas as pl
from jax.experimental.pallas import tpu as pltpu
from jax.sharding import PartitionSpec as P

MESH = pl.DeviceIdType.MESH
F32 = jnp.float32
BF16 = jnp.bfloat16

CH = 384
FRAMES = 4
TAPS = 3
LAYERS = 3
SPOTS = 96
ROWS = FRAMES * SPOTS
NX, NY, NZ = 4, 4, 8
KR = TAPS * CH
SL = KR // 8
UNIT = SL // 8
WIDTH_B = (256, 128, 256)


def cols(layer, path):
    wb = WIDTH_B[layer]
    return (wb, CH) if path == 0 else (0, wb)


def width(layer, path):
    lo, hi = cols(layer, path)
    return hi - lo


def task_of(y, z, c):
    return y * 16 + z * 2 + c


def unit_target(layer, unit):
    u = layer * 64 + unit
    return u // 3, u % 3


def kernel(*refs):
    it = iter(refs)
    take = lambda n: [next(it) for _ in range(n)]
    lat_hbm, cache_hbm, rg_hbm, w_hbm, bias_ref, sel_ref, dest_ref = take(7)
    latout_hbm, wg_ref = take(2)
    w_ref, e_ref, rg_ref, sp_ref, g_ref, dpad_ref, leave_ref, in_ref, latg_ref = take(9)
    gbuf = [take(2) for _ in range(LAYERS)]
    r1 = [take(2) for _ in range(LAYERS)]
    s2 = [take(2) for _ in range(LAYERS)]
    r2 = [take(2) for _ in range(LAYERS)]
    s3 = [take(2) for _ in range(LAYERS)]
    r3 = [take(2) for _ in range(LAYERS)]
    fs = [take(2) for _ in range(LAYERS)]
    (tmp_ref, mask_own, mask_ref, fin_ref) = take(4)
    (ld_sem, ch_s, ch_r, mk_s, mk_r, s1_s, s1_r, s2_s, s2_r, s3_s, s3_r, fn_s, fn_r, out_sem) = take(14)

    x = lax.axis_index("clip")
    pos = lax.axis_index("task")
    y = pos // 16
    z = (pos % 16) // 2
    c = pos % 2

    loads = {}
    def load(name, src, dst, k):
        loads[name] = pltpu.make_async_copy(src, dst, ld_sem.at[k])
        loads[name].start()
    load("lat", lat_hbm.at[0], e_ref.at[0, pl.ds(2, 4)], 0)
    for l in range(LAYERS):
        load(("c", l), cache_hbm.at[0, 0, l], e_ref.at[l, pl.ds(0, 2)], 1 + l)
        load(("w", l), w_hbm.at[l], w_ref.at[l], 4 + l)
    load("rg", rg_hbm.at[0], rg_ref, 7)

    def dev(xx, tt):
        return {"clip": xx, "task": tt}

    def b1(o):
        s = (2 * y + c + o) % 8
        return dev(x, task_of(s // 2, z, s % 2))

    def a1(o):
        s = (2 * x + c + o) % 8
        return dev(s // 2, task_of(y, z, s % 2))

    def px(o):
        return dev((x + o) % 4, pos)

    def py(o):
        return dev(x, task_of((y + o) % 4, z, c))

    def pz(o):
        return dev(x, task_of(y, (z + o) % 8, c))

    unit_b = 8 * (2 * y + c) + z
    unit_a = 8 * (2 * x + c) + 2 * y + z % 2

    def final_target(l, path):
        if path == 1:
            t, i = unit_target(l, unit_b)
            return x, t, i
        t, i = unit_target(l, unit_a)
        return z // 2, t, i

    def final_source(i, path):
        u = 3 * pos + i
        j = u % 64
        if path == 1:
            return x, task_of(j // 16, j % 8, (j // 8) % 2)
        return j // 16, task_of((j % 8) // 2, 2 * x + j % 2, (j // 8) % 2)

    barrier = pltpu.get_barrier_semaphore()
    greet = [b1(o) for o in range(1, 8)] + [a1(o) for o in range(1, 8)]
    greet += [px(o) for o in range(1, 4)] + [py(o) for o in range(1, 4)] + [pz(o) for o in range(1, 8)]
    greet += [dev(x, (pos + 1) % 64)]
    greet += [dev(*final_source(i, path)) for i in range(3) for path in range(2)]
    for who in greet:
        pl.semaphore_signal(barrier, inc=1, device_id=who, device_id_type=MESH)

    flag = jnp.max((sel_ref[...] == pos).astype(F32), axis=1, keepdims=True)
    mask = (lax.broadcasted_iota(jnp.int32, (8, 256), 0) == dest_ref[...]).astype(F32)
    mask_own[...] = mask
    mask_ref[1, 2 * y + c] = mask
    mask_ref[0, 2 * x + c] = mask
    dpad_ref[pl.ds(0, 2)] = jnp.zeros((2, SPOTS, CH), BF16)
    dpad_ref[pl.ds(6, 2)] = jnp.zeros((2, SPOTS, CH), BF16)

    @pl.when(pos == 63)
    def _():
        in_ref[...] = jnp.zeros(in_ref.shape, BF16)

    loads["lat"].wait()
    for l in range(LAYERS):
        loads[("c", l)].wait()
        loads[("w", l)].wait()
        lhs = jnp.concatenate([e_ref[l, k:k + 4].reshape(ROWS, CH) for k in range(TAPS)], axis=1)
        a = jnp.dot(lhs, w_ref[l].reshape(KR, CH), preferred_element_type=F32) + bias_ref[l:l + 1, :]
        sg = jax.nn.sigmoid(a)
        sp_ref[l] = sg * (1.0 + a * (1.0 - sg))
        if l < LAYERS - 1:
            h = e_ref[l, 2:6].reshape(ROWS, CH).astype(F32) + a * sg
            e_ref[l + 1, 2:6] = h.astype(BF16).reshape(FRAMES, SPOTS, CH)

    pl.semaphore_wait(barrier, len(greet))
    started = []

    def remote(src, dst, ssem, rsem, who):
        cp = pltpu.make_async_remote_copy(
            src_ref=src, dst_ref=dst, send_sem=ssem, recv_sem=rsem, device_id=who, device_id_type=MESH)
        cp.start()
        started.append(cp)
        return cp

    mk = {}
    for o in range(1, 8):
        mk[1, o] = remote(mask_own, mask_ref.at[1, 2 * y + c], mk_s.at[1, o], mk_r.at[1, o], b1(o))
        mk[0, o] = remote(mask_own, mask_ref.at[0, 2 * x + c], mk_s.at[0, o], mk_r.at[0, o], a1(o))

    loads["rg"].wait()
    g_ref[...] = rg_ref[...].reshape(ROWS, CH).astype(F32) * flag

    mine = [2 * x + c, 2 * y + c]
    first = [a1, b1]
    c1 = {}
    chain = {}
    for l in range(LAYERS - 1, -1, -1):
        if l < LAYERS - 1:
            @pl.when(pos < 63)
            def _(l=l):
                chain[l + 1].wait_recv()
            g_ref[pl.ds(192, 192)] += in_ref[l + 1].astype(F32)
        d = (g_ref[...] * sp_ref[l]).astype(BF16)
        dpad_ref[pl.ds(2, 4)] = d.reshape(FRAMES, SPOTS, CH)
        lhs = jnp.concatenate([dpad_ref[2:4].reshape(192, CH), dpad_ref[1:3].reshape(192, CH)], axis=1)
        rhs = jnp.concatenate([w_ref[l, 0], w_ref[l, 1]], axis=1)
        lead = lax.dot_general(lhs, rhs, (((1,), (1,)), ((), ())), preferred_element_type=F32)
        leave_ref[l] = lead.astype(BF16)
        chain[l] = pltpu.make_async_remote_copy(
            src_ref=leave_ref.at[l], dst_ref=in_ref.at[l], send_sem=ch_s.at[l], recv_sem=ch_r.at[l],
            device_id=dev(x, (pos + 63) % 64), device_id_type=MESH)

        @pl.when(pos > 0)
        def _(l=l):
            chain[l].start()

        pad = jnp.zeros((32, CH), BF16)
        et = jnp.concatenate([v for f in range(6) for v in (e_ref[l, f], pad)], axis=0).T
        et = jnp.concatenate([et[:, 128 * k:128 * k + 512] for k in range(TAPS)], axis=0)
        dp = jnp.concatenate([v for f in range(FRAMES) for v in (dpad_ref[2 + f], pad)], axis=0)
        for path in (1, 0):
            lo, hi = cols(l, path)
            grads = jnp.dot(et, dp[:, lo:hi], preferred_element_type=F32)
            gbuf[l][path][...] = grads.astype(BF16).reshape(8, SL, hi - lo)
            for o in range(1, 8):
                s = (mine[path] + o) % 8
                c1[l, path, o] = remote(
                    gbuf[l][path].at[s], r1[l][path].at[mine[path]],
                    s1_s.at[l, path, o], s1_r.at[l, path, o], first[path](o))
            r1[l][path][mine[path]] = gbuf[l][path][mine[path]]

        lhs = jnp.concatenate([dpad_ref[4 - k:8 - k].reshape(ROWS, CH) for k in range(TAPS)], axis=1)
        rhs = jnp.concatenate([w_ref[l, k] for k in range(TAPS)], axis=1)
        g_ref[...] += lax.dot_general(lhs, rhs, (((1,), (1,)), ((), ())), preferred_element_type=F32)

    @pl.when(pos < 63)
    def _():
        chain[0].wait_recv()
    g_ref[pl.ds(192, 192)] += in_ref[0].astype(F32)
    latg_ref[...] = g_ref[...].astype(BF16).reshape(FRAMES, SPOTS, CH)
    out_copy = pltpu.make_async_copy(latg_ref, latout_hbm.at[0], out_sem)
    out_copy.start()

    for cp in mk.values():
        cp.wait_recv()

    second = [py, px]
    here = [y, x]
    c2, c3 = {}, {}

    def stage1(l, path):
        w = width(l, path)
        for o in range(1, 8):
            c1[l, path, o].wait_recv()

        def step(i, _):
            rows = pl.ds(pl.multiple_of(i * 16, 16), 16)
            raw = [r1[l][path][s, rows, :].astype(F32) for s in range(8)]
            for r in range(4):
                tot = raw[0] * mask_ref[path, 0, r:r + 1, 0:w]
                for s in range(1, 8):
                    tot = tot + raw[s] * mask_ref[path, s, r:r + 1, 0:w]
                if path == 1:
                    s2[l][path][r, rows, :] = tot.astype(BF16)
                else:
                    tmp_ref[r, rows, 0:w] = tot
            return 0

        lax.fori_loop(0, SL // 16, step, 0)
        if path == 0:
            for yy in range(4):
                s2[l][path][yy] = jnp.concatenate(
                    [tmp_ref[r, 36 * yy:36 * yy + 36, 0:w] for r in range(4)], axis=0).astype(BF16)
        for o in range(1, 4):
            c2[l, path, o] = remote(
                s2[l][path].at[(here[path] + o) % 4], r2[l][path].at[here[path]],
                s2_s.at[l, path, o], s2_r.at[l, path, o], second[path](o))
        r2[l][path][here[path]] = s2[l][path][here[path]]

    def stage2(l, path):
        w = width(l, path)
        for o in range(1, 4):
            c2[l, path, o].wait_recv()
        tot = r2[l][path][0].astype(F32)
        for s in range(1, 4):
            tot = tot + r2[l][path][s].astype(F32)
        tot = jnp.concatenate([tot, jnp.zeros((16, w), F32)], axis=0)
        for zz in range(8):
            s3[l][path][zz] = tot[UNIT * zz:UNIT * zz + 32].astype(BF16)
        for o in range(1, 8):
            c3[l, path, o] = remote(
                s3[l][path].at[(z + o) % 8], r3[l][path].at[z],
                s3_s.at[l, path, o], s3_r.at[l, path, o], pz(o))
        r3[l][path][z] = s3[l][path][z]

    finals = []

    def stage3(l, path):
        lo, hi = cols(l, path)
        for o in range(1, 8):
            c3[l, path, o].wait_recv()
        tot = r3[l][path][0].astype(F32)
        for s in range(1, 8):
            tot = tot + r3[l][path][s].astype(F32)
        fs[l][path][...] = tot[0:24]
        xx, tt, i = final_target(l, path)
        own = jnp.logical_and(xx == x, tt == pos)
        dst = fin_ref.at[i, :, lo:hi]
        far = pltpu.make_async_remote_copy(
            src_ref=fs[l][path], dst_ref=dst, send_sem=fn_s.at[l, path], recv_sem=fn_r.at[i],
            device_id=dev(xx, tt), device_id_type=MESH)
        near = pltpu.make_async_copy(fs[l][path], dst, fn_r.at[i])

        @pl.when(own)
        def _():
            near.start()

        @pl.when(jnp.logical_not(own))
        def _():
            far.start()
        finals.append((own, far))

    for l in range(LAYERS - 1, -1, -1):
        for stage in (stage1, stage2, stage3):
            for path in (1, 0):
                stage(l, path)

    for i in range(3):
        pltpu.make_async_copy(fin_ref.at[i], fin_ref.at[i], fn_r.at[i]).wait()
    wg_ref[0] = jnp.concatenate([fin_ref[i, 0:UNIT] for i in range(3)], axis=0)

    for cp in started:
        cp.wait_send()
    for own, far in finals:
        @pl.when(jnp.logical_not(own))
        def _(far=far):
            far.wait_send()

    @pl.when(pos > 0)
    def _():
        for l in range(LAYERS):
            chain[l].wait_send()
    out_copy.wait()


def body(latents, caches, reward_grad, weights, biases, selected, destination):
    vmem = pltpu.VMEM
    per = lambda shape, kind: [vmem(shape(width(l, path)), kind) for l in range(LAYERS) for path in range(2)]
    scratch = [
        vmem((LAYERS, TAPS, CH, CH), BF16),
        vmem((LAYERS, 6, SPOTS, CH), BF16),
        vmem((FRAMES, SPOTS, CH), BF16),
        vmem((LAYERS, ROWS, CH), F32),
        vmem((ROWS, CH), F32),
        vmem((8, SPOTS, CH), BF16),
        vmem((LAYERS, 192, CH), BF16),
        vmem((LAYERS, 192, CH), BF16),
        vmem((FRAMES, SPOTS, CH), BF16),
    ]
    scratch += per(lambda w: (8, SL, w), BF16)
    scratch += per(lambda w: (8, SL, w), BF16)
    scratch += per(lambda w: (4, SL, w), BF16)
    scratch += per(lambda w: (4, SL, w), BF16)
    scratch += per(lambda w: (8, 32, w), BF16)
    scratch += per(lambda w: (8, 32, w), BF16)
    scratch += per(lambda w: (24, w), F32)
    scratch += [
        vmem((4, SL, 256), F32),
        vmem((8, 256), F32),
        vmem((2, 8, 8, 256), F32),
        vmem((3, 24, CH), F32),
    ]
    dma = pltpu.SemaphoreType.DMA
    scratch += [dma((8,)), dma((3,)), dma((3,)), dma((2, 8)), dma((2, 8))]
    scratch += [dma((3, 2, 8)), dma((3, 2, 8)), dma((3, 2, 4)), dma((3, 2, 4)), dma((3, 2, 8)), dma((3, 2, 8))]
    scratch += [dma((3, 2)), dma((3,)), dma(())]
    hbm = pl.BlockSpec(memory_space=pl.ANY)
    near = pl.BlockSpec(memory_space=pltpu.VMEM)
    return pl.pallas_call(
        kernel,
        out_shape=(
            jax.ShapeDtypeStruct((1, FRAMES, SPOTS, CH), BF16),
            jax.ShapeDtypeStruct((1, 3 * UNIT, CH), F32),
        ),
        in_specs=[hbm, hbm, hbm, hbm, near, near, near],
        out_specs=(hbm, near),
        scratch_shapes=scratch,
        compiler_params=pltpu.CompilerParams(
            collective_id=0, has_side_effects=True, vmem_limit_bytes=48 * 1024 * 1024),
        cost_estimate=pl.CostEstimate(flops=3_060_000_000, bytes_accessed=5_000_000, transcendentals=450_000),
    )(latents, caches, reward_grad, weights, biases, selected, destination)


def solution(mesh):
    in_specs = (
        P("clip", "task", None, None),
        P("clip", "task", None, None, None, None),
        P("clip", "task", None, None),
        P(),
        P(),
        P("clip", None),
        P("clip", "task"),
    )
    out_specs = (P("clip", "task", None, None), P("clip", "task", None))
    return jax.shard_map(body, mesh=mesh, in_specs=in_specs, out_specs=out_specs, check_vma=False)
```

```python
import jax
import jax.numpy as jnp
from jax import lax
from jax.experimental import pallas as pl
from jax.experimental.pallas import tpu as pltpu
from jax.sharding import PartitionSpec as P

MESH = pl.DeviceIdType.MESH
F32 = jnp.float32
BF16 = jnp.bfloat16

CH = 384
FRAMES = 4
TAPS = 3
LAYERS = 3
SPOTS = 96
ROWS = FRAMES * SPOTS
NX, NY, NZ = 4, 4, 8
KR = TAPS * CH
SL = KR // 8
UNIT = SL // 8
TOP = LAYERS - 1
WIDTH_B = (256, 128, 256)


def cols(layer, path):
    wb = WIDTH_B[layer]
    return (wb, CH) if path == 0 else (0, wb)


def width(layer, path):
    lo, hi = cols(layer, path)
    return hi - lo


def task_of(y, z, c):
    return y * 16 + z * 2 + c


def unit_target(layer, unit):
    u = layer * 64 + unit
    return u // 3, u % 3


def kernel(*refs):
    it = iter(refs)
    take = lambda n: [next(it) for _ in range(n)]
    lat_hbm, cache_hbm, rg_hbm, w_hbm, bias_ref, sel_ref, dest_ref = take(7)
    latout_hbm, wg_ref = take(2)
    w_ref, e_ref, rg_ref, sp_ref, g_ref, dpad_ref, leave_ref, in_ref, latg_ref = take(9)
    gbuf = [take(2) for _ in range(LAYERS)]
    r1 = [take(2) for _ in range(LAYERS)]
    s2 = [take(2) for _ in range(LAYERS)]
    r2 = [take(2) for _ in range(LAYERS)]
    s3 = take(LAYERS)
    r3 = take(LAYERS)
    fs = take(LAYERS)
    (tmp_ref, mask_ref, fin_ref) = take(3)
    (ld_sem, ch_s, ch_r, s1_s, s1_r, s2_s, s2_r, s3_s, s3_r, fn_s, fn_r, out_sem) = take(12)

    x = lax.axis_index("clip")
    pos = lax.axis_index("task")
    y = pos // 16
    z = (pos % 16) // 2
    c = pos % 2

    loads = {}
    def load(name, src, dst, k):
        loads[name] = pltpu.make_async_copy(src, dst, ld_sem.at[k])
        loads[name].start()
    load("lat", lat_hbm.at[0], e_ref.at[0, pl.ds(2, 4)], 0)
    for l in range(LAYERS):
        load(("c", l), cache_hbm.at[0, 0, l], e_ref.at[l, pl.ds(0, 2)], 1 + l)
        load(("w", l), w_hbm.at[l], w_ref.at[l], 4 + l)
    load("rg", rg_hbm.at[0], rg_ref, 7)

    def dev(xx, tt):
        return {"clip": xx, "task": tt}

    def b1(o):
        s = (2 * y + c + o) % 8
        return dev(x, task_of(s // 2, z, s % 2))

    def a1(o):
        s = (2 * x + c + o) % 8
        return dev(s // 2, task_of(y, z, s % 2))

    def px(o):
        return dev((x + o) % 4, pos)

    def py(o):
        return dev(x, task_of((y + o) % 4, z, c))

    def pz(o):
        return dev(x, task_of(y, (z + o) % 8, c))

    unit_b = 8 * (2 * y + c) + z
    unit_a = 8 * (2 * x + c) + 2 * y + z % 2

    def final_target(l, path):
        if path == 1:
            t, i = unit_target(l, unit_b)
            return x, t, i
        t, i = unit_target(l, unit_a)
        return z // 2, t, i

    def final_source(i, path):
        u = 3 * pos + i
        j = u % 64
        if path == 1:
            return x, task_of(j // 16, j % 8, (j // 8) % 2)
        return j // 16, task_of((j % 8) // 2, 2 * x + j % 2, (j // 8) % 2)

    barrier = pltpu.get_barrier_semaphore()
    greet = [b1(o) for o in range(1, 8)] + [a1(o) for o in range(1, 8)]
    greet += [px(o) for o in range(1, 4)] + [py(o) for o in range(1, 4)] + [pz(o) for o in range(1, 8)]
    greet += [dev(x, (pos + 1) % 64)]
    greet += [dev(*final_source(i, path)) for i in range(3) for path in range(2)]
    for who in greet:
        pl.semaphore_signal(barrier, inc=1, device_id=who, device_id_type=MESH)

    flag = jnp.max((sel_ref[...] == pos).astype(F32), axis=1, keepdims=True)
    for path in range(2):
        w = width(TOP, path)
        mask = (lax.broadcasted_iota(jnp.int32, (16, w), 0) == dest_ref[...]).astype(F32).astype(BF16)
        for s in range(8):
            gbuf[TOP][path][s, SL:SL + 16] = mask
    dpad_ref[pl.ds(0, 2)] = jnp.zeros((2, SPOTS, CH), BF16)
    dpad_ref[pl.ds(6, 2)] = jnp.zeros((2, SPOTS, CH), BF16)

    @pl.when(pos == 63)
    def _():
        in_ref[...] = jnp.zeros(in_ref.shape, BF16)

    loads["lat"].wait()
    for l in range(LAYERS):
        loads[("c", l)].wait()
        loads[("w", l)].wait()
        lhs = jnp.concatenate([e_ref[l, k:k + 4].reshape(ROWS, CH) for k in range(TAPS)], axis=1)
        a = jnp.dot(lhs, w_ref[l].reshape(KR, CH), preferred_element_type=F32) + bias_ref[l:l + 1, :]
        sg = jax.nn.sigmoid(a)
        sp_ref[l] = sg * (1.0 + a * (1.0 - sg))
        if l < LAYERS - 1:
            h = e_ref[l, 2:6].reshape(ROWS, CH).astype(F32) + a * sg
            e_ref[l + 1, 2:6] = h.astype(BF16).reshape(FRAMES, SPOTS, CH)

    pl.semaphore_wait(barrier, len(greet))
    started = []

    def remote(src, dst, ssem, rsem, who):
        cp = pltpu.make_async_remote_copy(
            src_ref=src, dst_ref=dst, send_sem=ssem, recv_sem=rsem, device_id=who, device_id_type=MESH)
        cp.start()
        started.append(cp)
        return cp

    loads["rg"].wait()
    g_ref[...] = rg_ref[...].reshape(ROWS, CH).astype(F32) * flag

    mine = [2 * x + c, 2 * y + c]
    first = [a1, b1]
    c1 = {}
    chain = {}
    for l in range(LAYERS - 1, -1, -1):
        if l < LAYERS - 1:
            @pl.when(pos < 63)
            def _(l=l):
                chain[l + 1].wait_recv()
            g_ref[pl.ds(192, 192)] += in_ref[l + 1].astype(F32)
        d = (g_ref[...] * sp_ref[l]).astype(BF16)
        dpad_ref[pl.ds(2, 4)] = d.reshape(FRAMES, SPOTS, CH)
        lhs = jnp.concatenate([dpad_ref[2:4].reshape(192, CH), dpad_ref[1:3].reshape(192, CH)], axis=1)
        rhs = jnp.concatenate([w_ref[l, 0], w_ref[l, 1]], axis=1)
        lead = lax.dot_general(lhs, rhs, (((1,), (1,)), ((), ())), preferred_element_type=F32)
        leave_ref[l] = lead.astype(BF16)
        chain[l] = pltpu.make_async_remote_copy(
            src_ref=leave_ref.at[l], dst_ref=in_ref.at[l], send_sem=ch_s.at[l], recv_sem=ch_r.at[l],
            device_id=dev(x, (pos + 63) % 64), device_id_type=MESH)

        @pl.when(pos > 0)
        def _(l=l):
            chain[l].start()

        pad = jnp.zeros((32, CH), BF16)
        et = jnp.concatenate([v for f in range(6) for v in (e_ref[l, f], pad)], axis=0).T
        et = jnp.concatenate([et[:, 128 * k:128 * k + 512] for k in range(TAPS)], axis=0)
        dp = jnp.concatenate([v for f in range(FRAMES) for v in (dpad_ref[2 + f], pad)], axis=0)
        for path in (1, 0):
            lo, hi = cols(l, path)
            grads = jnp.dot(et, dp[:, lo:hi], preferred_element_type=F32)
            gbuf[l][path][:, 0:SL] = grads.astype(BF16).reshape(8, SL, hi - lo)
            for o in range(1, 8):
                s = (mine[path] + o) % 8
                c1[l, path, o] = remote(
                    gbuf[l][path].at[s], r1[l][path].at[mine[path]],
                    s1_s.at[l, path, o], s1_r.at[l, path, o], first[path](o))
            r1[l][path][mine[path]] = gbuf[l][path][mine[path]]

        lhs = jnp.concatenate([dpad_ref[4 - k:8 - k].reshape(ROWS, CH) for k in range(TAPS)], axis=1)
        rhs = jnp.concatenate([w_ref[l, k] for k in range(TAPS)], axis=1)
        g_ref[...] += lax.dot_general(lhs, rhs, (((1,), (1,)), ((), ())), preferred_element_type=F32)

    out_copy = pltpu.make_async_copy(latg_ref, latout_hbm.at[0], out_sem)

    def latent_out():
        @pl.when(pos < 63)
        def _():
            chain[0].wait_recv()
        g_ref[pl.ds(192, 192)] += in_ref[0].astype(F32)
        latg_ref[...] = g_ref[...].astype(BF16).reshape(FRAMES, SPOTS, CH)
        out_copy.start()

    second = [py, px]
    here = [y, x]
    c2, c3 = {}, {}

    def stage1(l, path):
        w = width(l, path)
        for o in range(1, 8):
            c1[l, path, o].wait_recv()
        if l == TOP:
            for s in range(8):
                mask_ref[path, s] = r1[l][path][s, SL:SL + 16, 0:128].astype(F32)[0:8]

        def step(i, _):
            rows = pl.ds(pl.multiple_of(i * 16, 16), 16)
            for lane in range(0, w, 128):
                at = slice(lane, lane + 128)
                raw = [r1[l][path][s, rows, at].astype(F32) for s in range(8)]
                for r in range(4):
                    tot = raw[0] * mask_ref[path, 0, r:r + 1, :]
                    for s in range(1, 8):
                        tot = tot + raw[s] * mask_ref[path, s, r:r + 1, :]
                    if path == 1:
                        s2[l][path][r, rows, at] = tot.astype(BF16)
                    else:
                        tmp_ref[r, rows, at] = tot
            return 0

        lax.fori_loop(0, SL // 16, step, 0)
        if path == 0:
            for yy in range(4):
                s2[l][path][yy] = jnp.concatenate(
                    [tmp_ref[r, 36 * yy:36 * yy + 36, 0:w] for r in range(4)], axis=0).astype(BF16)
        for o in range(1, 4):
            c2[l, path, o] = remote(
                s2[l][path].at[(here[path] + o) % 4], r2[l][path].at[here[path]],
                s2_s.at[l, path, o], s2_r.at[l, path, o], second[path](o))
        r2[l][path][here[path]] = s2[l][path][here[path]]

    def stage2(l):
        tiles = [None] * 3
        for path in (1, 0):
            lo, hi = cols(l, path)
            for o in range(1, 4):
                c2[l, path, o].wait_recv()
            tot = r2[l][path][0].astype(F32)
            for s in range(1, 4):
                tot = tot + r2[l][path][s].astype(F32)
            for lane in range(lo, hi, 128):
                tiles[lane // 128] = tot[:, lane - lo:lane - lo + 128]
        fill = jnp.zeros((10, 128), F32)
        for zz in range(8):
            parts = [t[UNIT * zz:UNIT * zz + UNIT] for t in tiles]
            s3[l][zz] = jnp.concatenate(parts + [fill], axis=0).astype(BF16)
        for o in range(1, 8):
            c3[l, o] = remote(
                s3[l].at[(z + o) % 8], r3[l].at[z], s3_s.at[l, o], s3_r.at[l, o], pz(o))
        r3[l][z] = s3[l][z]

    finals = []

    def stage3(l):
        for o in range(1, 8):
            c3[l, o].wait_recv()
        tot = r3[l][0].astype(F32)
        for s in range(1, 8):
            tot = tot + r3[l][s].astype(F32)
        for ct in range(3):
            fs[l][ct] = tot[UNIT * ct:UNIT * ct + 24]
        for path in (1, 0):
            lo, hi = cols(l, path)
            tiles = pl.ds(lo // 128, (hi - lo) // 128)
            xx, tt, i = final_target(l, path)
            own = jnp.logical_and(xx == x, tt == pos)
            src, dst = fs[l].at[tiles], fin_ref.at[i, tiles]
            far = pltpu.make_async_remote_copy(
                src_ref=src, dst_ref=dst, send_sem=fn_s.at[l, path], recv_sem=fn_r.at[i],
                device_id=dev(xx, tt), device_id_type=MESH)
            near = pltpu.make_async_copy(src, dst, fn_r.at[i])

            @pl.when(own)
            def _():
                near.start()

            @pl.when(jnp.logical_not(own))
            def _():
                far.start()
            finals.append((own, far))

    stage1(2, 1)
    stage1(2, 0)
    stage1(1, 1)
    stage1(1, 0)
    stage2(2)
    latent_out()
    stage1(0, 1)
    stage1(0, 0)
    stage2(1)
    stage3(2)
    stage2(0)
    stage3(1)
    stage3(0)

    for i in range(3):
        pltpu.make_async_copy(fin_ref.at[i], fin_ref.at[i], fn_r.at[i]).wait()
    for ct in range(3):
        part = jnp.concatenate([fin_ref[i, ct, 0:UNIT] for i in range(3)], axis=0)
        wg_ref[:, 0, 128 * ct:128 * ct + 128] = part

    for cp in started:
        cp.wait_send()
    for own, far in finals:
        @pl.when(jnp.logical_not(own))
        def _(far=far):
            far.wait_send()

    @pl.when(pos > 0)
    def _():
        for l in range(LAYERS):
            chain[l].wait_send()
    out_copy.wait()


def body(latents, caches, reward_grad, weights, biases, selected, destination):
    vmem = pltpu.VMEM
    per = lambda shape, kind: [vmem(shape(width(l, path)), kind) for l in range(LAYERS) for path in range(2)]
    scratch = [
        vmem((LAYERS, TAPS, CH, CH), BF16),
        vmem((LAYERS, 6, SPOTS, CH), BF16),
        vmem((FRAMES, SPOTS, CH), BF16),
        vmem((LAYERS, ROWS, CH), F32),
        vmem((ROWS, CH), F32),
        vmem((8, SPOTS, CH), BF16),
        vmem((LAYERS, 192, CH), BF16),
        vmem((LAYERS, 192, CH), BF16),
        vmem((FRAMES, SPOTS, CH), BF16),
    ]
    slices = [vmem((8, SL + 16 * (l == TOP), width(l, path)), BF16) for l in range(LAYERS) for path in range(2)]
    scratch += slices + slices
    scratch += per(lambda w: (4, SL, w), BF16)
    scratch += per(lambda w: (4, SL, w), BF16)
    scratch += [vmem((8, 64, 128), BF16)] * LAYERS
    scratch += [vmem((8, 64, 128), BF16)] * LAYERS
    scratch += [vmem((3, 24, 128), F32)] * LAYERS
    scratch += [vmem((4, SL, 256), F32), vmem((2, 8, 8, 128), F32), vmem((3, 3, 24, 128), F32)]
    dma = pltpu.SemaphoreType.DMA
    scratch += [dma((8,)), dma((3,)), dma((3,))]
    scratch += [dma((3, 2, 8)), dma((3, 2, 8)), dma((3, 2, 4)), dma((3, 2, 4)), dma((3, 8)), dma((3, 8))]
    scratch += [dma((3, 2)), dma((3,)), dma(())]
    hbm = pl.BlockSpec(memory_space=pl.ANY)
    near = pl.BlockSpec(memory_space=pltpu.VMEM)
    latent_grad, block = pl.pallas_call(
        kernel,
        out_shape=(
            jax.ShapeDtypeStruct((1, FRAMES, SPOTS, CH), BF16),
            jax.ShapeDtypeStruct((3 * UNIT, 1, CH), F32),
        ),
        in_specs=[hbm, hbm, hbm, hbm, near, near, near],
        out_specs=(hbm, near),
        scratch_shapes=scratch,
        compiler_params=pltpu.CompilerParams(
            collective_id=0, has_side_effects=True, vmem_limit_bytes=63 * 1024 * 1024),
        cost_estimate=pl.CostEstimate(flops=3_060_000_000, bytes_accessed=5_000_000, transcendentals=450_000),
    )(latents, caches, reward_grad, weights, biases, selected, destination)
    return latent_grad, jnp.transpose(block, (1, 0, 2))


def solution(mesh):
    in_specs = (
        P("clip", "task", None, None),
        P("clip", "task", None, None, None, None),
        P("clip", "task", None, None),
        P(),
        P(),
        P("clip", None),
        P("clip", "task"),
    )
    out_specs = (P("clip", "task", None, None), P("clip", "task", None))
    return jax.shard_map(body, mesh=mesh, in_specs=in_specs, out_specs=out_specs, check_vma=False)
```

```python
import jax
import jax.numpy as jnp
from jax import lax
from jax.experimental import pallas as pl
from jax.experimental.pallas import tpu as pltpu
from jax.sharding import PartitionSpec as P

MESH = pl.DeviceIdType.MESH
F32 = jnp.float32
BF16 = jnp.bfloat16

CH = 384
FRAMES = 4
TAPS = 3
LAYERS = 3
SPOTS = 96
ROWS = FRAMES * SPOTS
NX, NY, NZ = 4, 4, 8
KR = TAPS * CH
SL = KR // 8
UNIT = SL // 8
TOP = LAYERS - 1
WIDTH_B = (256, 128, 256)


def cols(layer, path):
    wb = WIDTH_B[layer]
    return (wb, CH) if path == 0 else (0, wb)


def width(layer, path):
    lo, hi = cols(layer, path)
    return hi - lo


def task_of(y, z, c):
    return y * 16 + z * 2 + c


def unit_target(layer, unit):
    u = layer * 64 + unit
    return u // 3, u % 3


def kernel(*refs):
    it = iter(refs)
    take = lambda n: [next(it) for _ in range(n)]
    lat_hbm, cache_hbm, rg_hbm, w_hbm, bias_hbm, sel_hbm, dest_hbm = take(7)
    latout_hbm, fin_ref = take(2)
    w_ref, e_ref, rg_ref, sp_ref, g_ref, dpad_ref, leave_ref, in_ref, latg_ref = take(9)
    gbuf = [take(2) for _ in range(LAYERS)]
    r1 = [take(2) for _ in range(LAYERS)]
    s2 = [take(2) for _ in range(LAYERS)]
    r2 = [take(2) for _ in range(LAYERS)]
    s3 = take(LAYERS)
    r3 = take(LAYERS)
    fs = take(LAYERS)
    (tmp_ref, mask_ref, bias_ref, sel_ref, dest_ref) = take(5)
    (ld_sem, ch_s, ch_r, s1_s, s1_r, s2_s, s2_r, s3_s, s3_r, fn_s, fn_r, out_sem) = take(12)

    x = lax.axis_index("clip")
    pos = lax.axis_index("task")
    y = pos // 16
    z = (pos % 16) // 2
    c = pos % 2

    loads = {}
    def load(name, src, dst, k):
        loads[name] = pltpu.make_async_copy(src, dst, ld_sem.at[k])
        loads[name].start()
    load("sel", sel_hbm, sel_ref, 8)
    load("dest", dest_hbm, dest_ref, 9)
    load("bias", bias_hbm, bias_ref, 10)
    load("lat", lat_hbm.at[0], e_ref.at[0, pl.ds(2, 4)], 0)
    for l in range(LAYERS):
        load(("c", l), cache_hbm.at[0, 0, l], e_ref.at[l, pl.ds(0, 2)], 1 + l)
        load(("w", l), w_hbm.at[l], w_ref.at[l], 4 + l)
    load("rg", rg_hbm.at[0], rg_ref, 7)

    def dev(xx, tt):
        return {"clip": xx, "task": tt}

    def b1(o):
        s = (2 * y + c + o) % 8
        return dev(x, task_of(s // 2, z, s % 2))

    def a1(o):
        s = (2 * x + c + o) % 8
        return dev(s // 2, task_of(y, z, s % 2))

    def px(o):
        return dev((x + o) % 4, pos)

    def py(o):
        return dev(x, task_of((y + o) % 4, z, c))

    def pz(o):
        return dev(x, task_of(y, (z + o) % 8, c))

    unit_b = 8 * (2 * y + c) + z
    unit_a = 8 * (2 * x + c) + 2 * y + z % 2

    def final_target(l, path):
        if path == 1:
            t, i = unit_target(l, unit_b)
            return x, t, i
        t, i = unit_target(l, unit_a)
        return z // 2, t, i

    def final_source(i, path):
        u = 3 * pos + i
        j = u % 64
        if path == 1:
            return x, task_of(j // 16, j % 8, (j // 8) % 2)
        return j // 16, task_of((j % 8) // 2, 2 * x + j % 2, (j // 8) % 2)

    barrier = pltpu.get_barrier_semaphore()
    greet = [b1(o) for o in range(1, 8)] + [a1(o) for o in range(1, 8)]
    greet += [px(o) for o in range(1, 4)] + [py(o) for o in range(1, 4)] + [pz(o) for o in range(1, 8)]
    greet += [dev(x, (pos + 1) % 64)]
    greet += [dev(*final_source(i, path)) for i in range(3) for path in range(2)]
    for who in greet:
        pl.semaphore_signal(barrier, inc=1, device_id=who, device_id_type=MESH)

    for name in ("sel", "dest", "bias"):
        loads[name].wait()
    flag = jnp.max((sel_ref[...] == pos).astype(F32), axis=1, keepdims=True)
    for path in range(2):
        w = width(TOP, path)
        mask = (lax.broadcasted_iota(jnp.int32, (16, w), 0) == dest_ref[...]).astype(F32).astype(BF16)
        for s in range(8):
            gbuf[TOP][path][s, SL:SL + 16] = mask
    dpad_ref[pl.ds(0, 2)] = jnp.zeros((2, SPOTS, CH), BF16)
    dpad_ref[pl.ds(6, 2)] = jnp.zeros((2, SPOTS, CH), BF16)

    @pl.when(pos == 63)
    def _():
        in_ref[...] = jnp.zeros(in_ref.shape, BF16)

    loads["lat"].wait()
    for l in range(LAYERS):
        loads[("c", l)].wait()
        loads[("w", l)].wait()
        lhs = jnp.concatenate([e_ref[l, k:k + 4].reshape(ROWS, CH) for k in range(TAPS)], axis=1)
        a = jnp.dot(lhs, w_ref[l].reshape(KR, CH), preferred_element_type=F32) + bias_ref[l:l + 1, :]
        sg = jax.nn.sigmoid(a)
        sp_ref[l] = sg * (1.0 + a * (1.0 - sg))
        if l < LAYERS - 1:
            h = e_ref[l, 2:6].reshape(ROWS, CH).astype(F32) + a * sg
            e_ref[l + 1, 2:6] = h.astype(BF16).reshape(FRAMES, SPOTS, CH)

    pl.semaphore_wait(barrier, len(greet))
    started = []

    def remote(src, dst, ssem, rsem, who):
        cp = pltpu.make_async_remote_copy(
            src_ref=src, dst_ref=dst, send_sem=ssem, recv_sem=rsem, device_id=who, device_id_type=MESH)
        cp.start()
        started.append(cp)
        return cp

    loads["rg"].wait()
    g_ref[...] = rg_ref[...].reshape(ROWS, CH).astype(F32) * flag

    mine = [2 * x + c, 2 * y + c]
    first = [a1, b1]
    c1 = {}
    chain = {}
    def send1(l, path):
        for o in range(1, 8):
            s = (mine[path] + o) % 8
            c1[l, path, o] = remote(
                gbuf[l][path].at[s], r1[l][path].at[mine[path]],
                s1_s.at[l, path, o], s1_r.at[l, path, o], first[path](o))
        r1[l][path][mine[path]] = gbuf[l][path][mine[path]]

    for l in range(LAYERS - 1, -1, -1):
        if l < LAYERS - 1:
            @pl.when(pos < 63)
            def _(l=l):
                chain[l + 1].wait_recv()
            g_ref[pl.ds(192, 192)] += in_ref[l + 1].astype(F32)
        d = (g_ref[...] * sp_ref[l]).astype(BF16)
        dpad_ref[pl.ds(2, 4)] = d.reshape(FRAMES, SPOTS, CH)
        lhs = jnp.concatenate([dpad_ref[2:4].reshape(192, CH), dpad_ref[1:3].reshape(192, CH)], axis=1)
        rhs = jnp.concatenate([w_ref[l, 0], w_ref[l, 1]], axis=1)
        lead = lax.dot_general(lhs, rhs, (((1,), (1,)), ((), ())), preferred_element_type=F32)
        leave_ref[l] = lead.astype(BF16)
        chain[l] = pltpu.make_async_remote_copy(
            src_ref=leave_ref.at[l], dst_ref=in_ref.at[l], send_sem=ch_s.at[l], recv_sem=ch_r.at[l],
            device_id=dev(x, (pos + 63) % 64), device_id_type=MESH)

        @pl.when(pos > 0)
        def _(l=l):
            chain[l].start()

        pad = jnp.zeros((32, CH), BF16)
        et = jnp.concatenate([v for f in range(6) for v in (e_ref[l, f], pad)], axis=0).T
        et = jnp.concatenate([et[:, 128 * k:128 * k + 512] for k in range(TAPS)], axis=0)
        dp = jnp.concatenate([v for f in range(FRAMES) for v in (dpad_ref[2 + f], pad)], axis=0)
        for path in (1, 0):
            lo, hi = cols(l, path)
            grads = jnp.dot(et, dp[:, lo:hi], preferred_element_type=F32)
            gbuf[l][path][:, 0:SL] = grads.astype(BF16).reshape(8, SL, hi - lo)
            if l != 1:
                send1(l, path)
        if l == 0:
            send1(1, 1)
            send1(1, 0)

        lhs = jnp.concatenate([dpad_ref[4 - k:8 - k].reshape(ROWS, CH) for k in range(TAPS)], axis=1)
        rhs = jnp.concatenate([w_ref[l, k] for k in range(TAPS)], axis=1)
        g_ref[...] += lax.dot_general(lhs, rhs, (((1,), (1,)), ((), ())), preferred_element_type=F32)

    out_copy = pltpu.make_async_copy(latg_ref, latout_hbm.at[0], out_sem)

    def latent_out():
        @pl.when(pos < 63)
        def _():
            chain[0].wait_recv()
        g_ref[pl.ds(192, 192)] += in_ref[0].astype(F32)
        latg_ref[...] = g_ref[...].astype(BF16).reshape(FRAMES, SPOTS, CH)
        out_copy.start()

    second = [py, px]
    here = [y, x]
    c2, c3 = {}, {}

    def stage1(l, path):
        w = width(l, path)
        for o in range(1, 8):
            c1[l, path, o].wait_recv()
        if l == TOP:
            for s in range(8):
                mask_ref[path, s] = r1[l][path][s, SL:SL + 16, 0:128].astype(F32)[0:8]

        def step(i, _):
            rows = pl.ds(pl.multiple_of(i * 16, 16), 16)
            for lane in range(0, w, 128):
                at = slice(lane, lane + 128)
                raw = [r1[l][path][s, rows, at].astype(F32) for s in range(8)]
                for r in range(4):
                    tot = raw[0] * mask_ref[path, 0, r:r + 1, :]
                    for s in range(1, 8):
                        tot = tot + raw[s] * mask_ref[path, s, r:r + 1, :]
                    if path == 1:
                        s2[l][path][r, rows, at] = tot.astype(BF16)
                    else:
                        tmp_ref[r, rows, at] = tot
            return 0

        lax.fori_loop(0, SL // 16, step, 0)
        if path == 0:
            for yy in range(4):
                s2[l][path][yy] = jnp.concatenate(
                    [tmp_ref[r, 36 * yy:36 * yy + 36, 0:w] for r in range(4)], axis=0).astype(BF16)
        for o in range(1, 4):
            c2[l, path, o] = remote(
                s2[l][path].at[(here[path] + o) % 4], r2[l][path].at[here[path]],
                s2_s.at[l, path, o], s2_r.at[l, path, o], second[path](o))
        r2[l][path][here[path]] = s2[l][path][here[path]]

    def stage2(l):
        tiles = [None] * 3
        for path in (1, 0):
            lo, hi = cols(l, path)
            for o in range(1, 4):
                c2[l, path, o].wait_recv()
            tot = r2[l][path][0].astype(F32)
            for s in range(1, 4):
                tot = tot + r2[l][path][s].astype(F32)
            for lane in range(lo, hi, 128):
                tiles[lane // 128] = tot[:, lane - lo:lane - lo + 128]
        fill = jnp.zeros((10, 128), F32)
        for zz in range(8):
            parts = [t[UNIT * zz:UNIT * zz + UNIT] for t in tiles]
            s3[l][zz] = jnp.concatenate(parts + [fill], axis=0).astype(BF16)
        for o in range(1, 8):
            c3[l, o] = remote(
                s3[l].at[(z + o) % 8], r3[l].at[z], s3_s.at[l, o], s3_r.at[l, o], pz(o))
        r3[l][z] = s3[l][z]

    finals = []

    def stage3(l):
        for o in range(1, 8):
            c3[l, o].wait_recv()
        tot = r3[l][0].astype(F32)
        for s in range(1, 8):
            tot = tot + r3[l][s].astype(F32)
        for ct in range(3):
            fs[l][ct] = tot[UNIT * ct:UNIT * ct + 24]
        for path in (1, 0):
            lo, hi = cols(l, path)
            tiles = pl.ds(lo // 128, (hi - lo) // 128)
            xx, tt, i = final_target(l, path)
            own = jnp.logical_and(xx == x, tt == pos)
            src, dst = fs[l].at[tiles], fin_ref.at[i, tiles]
            far = pltpu.make_async_remote_copy(
                src_ref=src, dst_ref=dst, send_sem=fn_s.at[l, path], recv_sem=fn_r.at[i],
                device_id=dev(xx, tt), device_id_type=MESH)
            near = pltpu.make_async_copy(src, dst, fn_r.at[i])

            @pl.when(own)
            def _():
                near.start()

            @pl.when(jnp.logical_not(own))
            def _():
                far.start()
            finals.append((own, far))

    stage1(2, 1)
    stage1(2, 0)
    latent_out()
    stage1(0, 1)
    stage1(0, 0)
    stage2(2)
    stage1(1, 1)
    stage1(1, 0)
    stage2(0)
    stage3(2)
    stage2(1)
    stage3(0)
    stage3(1)

    for i in range(3):
        pltpu.make_async_copy(fin_ref.at[i], fin_ref.at[i], fn_r.at[i]).wait()
    for cp in started:
        cp.wait_send()
    for own, far in finals:
        @pl.when(jnp.logical_not(own))
        def _(far=far):
            far.wait_send()

    @pl.when(pos > 0)
    def _():
        for l in range(LAYERS):
            chain[l].wait_send()
    out_copy.wait()


def finish(lat_ref, unit_ref, latout_ref, wg_ref):
    latout_ref[...] = lat_ref[...]
    for ct in range(3):
        part = jnp.concatenate([unit_ref[i, ct, 0:UNIT] for i in range(3)], axis=0)
        wg_ref[:, 0, 128 * ct:128 * ct + 128] = part


def body(latents, caches, reward_grad, weights, biases, selected, destination):
    vmem = pltpu.VMEM
    per = lambda shape, kind: [vmem(shape(width(l, path)), kind) for l in range(LAYERS) for path in range(2)]
    scratch = [
        vmem((LAYERS, TAPS, CH, CH), BF16),
        vmem((LAYERS, 6, SPOTS, CH), BF16),
        vmem((FRAMES, SPOTS, CH), BF16),
        vmem((LAYERS, ROWS, CH), F32),
        vmem((ROWS, CH), F32),
        vmem((8, SPOTS, CH), BF16),
        vmem((LAYERS, 192, CH), BF16),
        vmem((LAYERS, 192, CH), BF16),
        vmem((FRAMES, SPOTS, CH), BF16),
    ]
    slices = [vmem((8, SL + 16 * (l == TOP), width(l, path)), BF16) for l in range(LAYERS) for path in range(2)]
    scratch += slices + slices
    scratch += per(lambda w: (4, SL, w), BF16)
    scratch += per(lambda w: (4, SL, w), BF16)
    scratch += [vmem((8, 64, 128), BF16)] * LAYERS
    scratch += [vmem((8, 64, 128), BF16)] * LAYERS
    scratch += [vmem((3, 24, 128), F32)] * LAYERS
    scratch += [vmem((4, SL, 256), F32), vmem((2, 8, 8, 128), F32)]
    scratch += [vmem((LAYERS, CH), F32), vmem((1, 32), jnp.int32), vmem((1, 1), jnp.int32)]
    dma = pltpu.SemaphoreType.DMA
    scratch += [dma((11,)), dma((3,)), dma((3,))]
    scratch += [dma((3, 2, 8)), dma((3, 2, 8)), dma((3, 2, 4)), dma((3, 2, 4)), dma((3, 8)), dma((3, 8))]
    scratch += [dma((3, 2)), dma((3,)), dma(())]
    hbm = pl.BlockSpec(memory_space=pl.ANY)
    near = pl.BlockSpec(memory_space=pltpu.VMEM)
    latent_grad, units = pl.pallas_call(
        kernel,
        out_shape=(
            jax.ShapeDtypeStruct((1, FRAMES, SPOTS, CH), BF16),
            jax.ShapeDtypeStruct((3, 3, 24, 128), F32),
        ),
        in_specs=[hbm] * 7,
        out_specs=(hbm, hbm),
        scratch_shapes=scratch,
        compiler_params=pltpu.CompilerParams(
            collective_id=0, has_side_effects=True, vmem_limit_bytes=63 * 1024 * 1024),
        cost_estimate=pl.CostEstimate(flops=3_060_000_000, bytes_accessed=5_000_000, transcendentals=450_000),
    )(latents, caches, reward_grad, weights, biases, selected, destination)
    latent_grad, block = pl.pallas_call(
        finish,
        out_shape=(
            jax.ShapeDtypeStruct((1, FRAMES, SPOTS, CH), BF16),
            jax.ShapeDtypeStruct((3 * UNIT, 1, CH), F32),
        ),
        in_specs=[near, near],
        out_specs=(near, near),
    )(latent_grad, units)
    return latent_grad, jnp.transpose(block, (1, 0, 2))


def solution(mesh):
    in_specs = (
        P("clip", "task", None, None),
        P("clip", "task", None, None, None, None),
        P("clip", "task", None, None),
        P(),
        P(),
        P("clip", None),
        P("clip", "task"),
    )
    out_specs = (P("clip", "task", None, None), P("clip", "task", None))
    return jax.shard_map(body, mesh=mesh, in_specs=in_specs, out_specs=out_specs, check_vma=False)
```

```python
import jax
import jax.numpy as jnp
from jax import lax
from jax.experimental import pallas as pl
from jax.experimental.pallas import tpu as pltpu
from jax.sharding import PartitionSpec as P

MESH = pl.DeviceIdType.MESH
F32 = jnp.float32
BF16 = jnp.bfloat16

CH = 384
FRAMES = 4
TAPS = 3
LAYERS = 3
SPOTS = 96
ROWS = FRAMES * SPOTS
NX, NY, NZ = 4, 4, 8
KR = TAPS * CH
SL = KR // 8
UNIT = SL // 8
TOP = LAYERS - 1
WIDTH_B = (256, 128, 256)


def cols(layer, path):
    wb = WIDTH_B[layer]
    return (wb, CH) if path == 0 else (0, wb)


def width(layer, path):
    lo, hi = cols(layer, path)
    return hi - lo


def task_of(y, z, c):
    return y * 16 + z * 2 + c


def kernel(*refs):
    it = iter(refs)
    take = lambda n: [next(it) for _ in range(n)]
    lat_hbm, cache_hbm, rg_hbm, w_hbm, bias_hbm, sel_hbm, dest_hbm = take(7)
    latout_hbm, fin_ref = take(2)
    w_ref, e_ref, rg_ref, sp_ref, g_ref, dpad_ref, leave_ref, in_ref, latg_ref = take(9)
    gbuf = [take(2) for _ in range(LAYERS)]
    r1 = [take(2) for _ in range(LAYERS)]
    s2 = [take(2) for _ in range(LAYERS)]
    r2 = [take(2) for _ in range(LAYERS)]
    s3 = take(LAYERS)
    r3 = take(LAYERS)
    fs = take(LAYERS)
    (mask_ref, bias_ref, sel_ref, dest_ref) = take(4)
    (ld_sem, ch_s, ch_r, s1_s, s1_r, s2_s, s2_r, s3_s, s3_r, fn_s, fn_r, out_sem) = take(12)

    x = lax.axis_index("clip")
    pos = lax.axis_index("task")
    y = pos // 16
    z = (pos % 16) // 2
    c = pos % 2

    loads = {}
    def load(name, src, dst, k):
        loads[name] = pltpu.make_async_copy(src, dst, ld_sem.at[k])
        loads[name].start()
    load("sel", sel_hbm, sel_ref, 8)
    load("dest", dest_hbm, dest_ref, 9)
    load("bias", bias_hbm, bias_ref, 10)
    load("lat", lat_hbm.at[0], e_ref.at[0, pl.ds(2, 4)], 0)
    for l in range(LAYERS):
        load(("c", l), cache_hbm.at[0, 0, l], e_ref.at[l, pl.ds(0, 2)], 1 + l)
        load(("w", l), w_hbm.at[l], w_ref.at[l], 4 + l)
    load("rg", rg_hbm.at[0], rg_ref, 7)

    def dev(xx, tt):
        return {"clip": xx, "task": tt}

    def b1(o):
        s = (2 * y + c + o) % 8
        return dev(x, task_of(s // 2, z, s % 2))

    def a1(o):
        s = (2 * x + c + o) % 8
        return dev(s // 2, task_of(y, z, s % 2))

    def px(o):
        return dev((x + o) % 4, pos)

    def py(o):
        return dev(x, task_of((y + o) % 4, z, c))

    def pz(o):
        return dev(x, task_of(y, (z + o) % 8, c))

    place1 = [2 * x + c, 2 * y + c]
    replica = [y, x]

    def z_shift(l):
        return 2 + 2 * l + l // 2

    def owner(l, path):
        u = 64 * l + 8 * ((z - z_shift(l) + 8) % 8) + place1[path]
        return replica[path], u // 3, u % 3

    def source(i, path):
        u = 3 * pos + i
        l, m, s = u // 64, (u % 64) // 8, u % 8
        zz = (m + z_shift(l)) % 8
        if path == 1:
            return dev(x, task_of(s // 2, zz, s % 2))
        return dev(s // 2, task_of(x, zz, s % 2))

    barrier = pltpu.get_barrier_semaphore()
    greet = [b1(o) for o in range(1, 8)] + [a1(o) for o in range(1, 8)]
    greet += [px(o) for o in range(1, 4)] + [py(o) for o in range(1, 4)] + [pz(o) for o in range(1, 8)]
    greet += [dev(x, (pos + 1) % 64)]
    greet += [source(i, path) for i in range(3) for path in range(2)]
    for who in greet:
        pl.semaphore_signal(barrier, inc=1, device_id=who, device_id_type=MESH)

    for name in ("sel", "dest", "bias"):
        loads[name].wait()
    flag = jnp.max((sel_ref[...] == pos).astype(F32), axis=1, keepdims=True)
    for path in range(2):
        w = width(TOP, path)
        mask = (lax.broadcasted_iota(jnp.int32, (16, w), 0) == dest_ref[...]).astype(F32).astype(BF16)
        for s in range(8):
            gbuf[TOP][path][s, SL:SL + 16] = mask
    dpad_ref[pl.ds(0, 2)] = jnp.zeros((2, SPOTS, CH), BF16)
    dpad_ref[pl.ds(6, 2)] = jnp.zeros((2, SPOTS, CH), BF16)

    @pl.when(pos == 63)
    def _():
        in_ref[...] = jnp.zeros(in_ref.shape, BF16)

    loads["lat"].wait()
    for l in range(LAYERS):
        loads[("c", l)].wait()
        loads[("w", l)].wait()
        lhs = jnp.concatenate([e_ref[l, k:k + 4].reshape(ROWS, CH) for k in range(TAPS)], axis=1)
        a = jnp.dot(lhs, w_ref[l].reshape(KR, CH), preferred_element_type=F32) + bias_ref[l:l + 1, :]
        sg = jax.nn.sigmoid(a)
        sp_ref[l] = sg * (1.0 + a * (1.0 - sg))
        if l < LAYERS - 1:
            h = e_ref[l, 2:6].reshape(ROWS, CH).astype(F32) + a * sg
            e_ref[l + 1, 2:6] = h.astype(BF16).reshape(FRAMES, SPOTS, CH)

    pl.semaphore_wait(barrier, len(greet))
    started = []

    def remote(src, dst, ssem, rsem, who):
        cp = pltpu.make_async_remote_copy(
            src_ref=src, dst_ref=dst, send_sem=ssem, recv_sem=rsem, device_id=who, device_id_type=MESH)
        cp.start()
        started.append(cp)
        return cp

    loads["rg"].wait()
    g_ref[...] = rg_ref[...].reshape(ROWS, CH).astype(F32) * flag

    mine = place1
    first = [a1, b1]
    c1 = {}
    chain = {}
    def send1(l, path):
        for o in range(1, 8):
            s = (mine[path] + o) % 8
            c1[l, path, o] = remote(
                gbuf[l][path].at[s], r1[l][path].at[mine[path]],
                s1_s.at[l, path, o], s1_r.at[l, path, o], first[path](o))
        r1[l][path][mine[path]] = gbuf[l][path][mine[path]]

    for l in range(LAYERS - 1, -1, -1):
        if l < LAYERS - 1:
            @pl.when(pos < 63)
            def _(l=l):
                chain[l + 1].wait_recv()
            g_ref[pl.ds(192, 192)] += in_ref[l + 1].astype(F32)
        d = (g_ref[...] * sp_ref[l]).astype(BF16)
        dpad_ref[pl.ds(2, 4)] = d.reshape(FRAMES, SPOTS, CH)
        def lead_out(l=l, d=d):
            lhs = jnp.concatenate([dpad_ref[2:4].reshape(192, CH), dpad_ref[1:3].reshape(192, CH)], axis=1)
            rhs = jnp.concatenate([w_ref[l, 0], w_ref[l, 1]], axis=1)
            lead = lax.dot_general(lhs, rhs, (((1,), (1,)), ((), ())), preferred_element_type=F32)
            leave_ref[l] = lead.astype(BF16)
            chain[l] = pltpu.make_async_remote_copy(
                src_ref=leave_ref.at[l], dst_ref=in_ref.at[l], send_sem=ch_s.at[l], recv_sem=ch_r.at[l],
                device_id=dev(x, (pos + 63) % 64), device_id_type=MESH)

            @pl.when(pos > 0)
            def _(l=l):
                chain[l].start()

        def kernel_grad(l=l):
            pad = jnp.zeros((32, CH), BF16)
            et = jnp.concatenate([v for f in range(6) for v in (e_ref[l, f], pad)], axis=0).T
            et = jnp.concatenate([et[:, 128 * k:128 * k + 512] for k in range(TAPS)], axis=0)
            dp = jnp.concatenate([v for f in range(FRAMES) for v in (dpad_ref[2 + f], pad)], axis=0)
            for path in (1, 0):
                lo, hi = cols(l, path)
                grads = jnp.dot(et, dp[:, lo:hi], preferred_element_type=F32)
                for s in range(8):
                    rows = [grads[SL * m + UNIT * s:SL * m + UNIT * s + UNIT] for m in range(8)]
                    gbuf[l][path][s, 0:SL] = jnp.concatenate(rows, axis=0).astype(BF16)
                if l != 1:
                    send1(l, path)
        if l == LAYERS - 1:
            kernel_grad()
            lead_out()
        else:
            lead_out()
            kernel_grad()
        if l == 0:
            send1(1, 1)
            send1(1, 0)

        lhs = jnp.concatenate([dpad_ref[4 - k:8 - k].reshape(ROWS, CH) for k in range(TAPS)], axis=1)
        rhs = jnp.concatenate([w_ref[l, k] for k in range(TAPS)], axis=1)
        g_ref[...] += lax.dot_general(lhs, rhs, (((1,), (1,)), ((), ())), preferred_element_type=F32)

    out_copy = pltpu.make_async_copy(latg_ref, latout_hbm.at[0], out_sem)

    def latent_out():
        @pl.when(pos < 63)
        def _():
            chain[0].wait_recv()
        g_ref[pl.ds(192, 192)] += in_ref[0].astype(F32)
        latg_ref[...] = g_ref[...].astype(BF16).reshape(FRAMES, SPOTS, CH)
        out_copy.start()

    second = [py, px]
    here = [y, x]
    c2, c3 = {}, {}

    def stage1(l, path):
        w = width(l, path)
        for o in range(1, 8):
            c1[l, path, o].wait_recv()
        if l == TOP:
            for s in range(8):
                mask_ref[path, s] = r1[l][path][s, SL:SL + 16, 0:128].astype(F32)[0:8]

        def step(i, _):
            rows = pl.ds(pl.multiple_of(i * 16, 16), 16)
            for lane in range(0, w, 128):
                at = slice(lane, lane + 128)
                raw = [r1[l][path][s, rows, at].astype(F32) for s in range(8)]
                for r in range(4):
                    tot = raw[0] * mask_ref[path, 0, r:r + 1, :]
                    for s in range(1, 8):
                        tot = tot + raw[s] * mask_ref[path, s, r:r + 1, :]
                    s2[l][path][r, rows, at] = tot.astype(BF16)
            return 0

        lax.fori_loop(0, SL // 16, step, 0)
        for o in range(1, 4):
            c2[l, path, o] = remote(
                s2[l][path].at[(here[path] + o) % 4], r2[l][path].at[here[path]],
                s2_s.at[l, path, o], s2_r.at[l, path, o], second[path](o))
        r2[l][path][here[path]] = s2[l][path][here[path]]

    def stage2(l):
        tiles = [None] * 3
        for path in (1, 0):
            lo, hi = cols(l, path)
            for o in range(1, 4):
                c2[l, path, o].wait_recv()
            tot = r2[l][path][0].astype(F32)
            for s in range(1, 4):
                tot = tot + r2[l][path][s].astype(F32)
            for lane in range(lo, hi, 128):
                tiles[lane // 128] = tot[:, lane - lo:lane - lo + 128]
        fill = jnp.zeros((10, 128), F32)
        for m in range(8):
            parts = [t[UNIT * m:UNIT * m + UNIT] for t in tiles]
            s3[l][m] = jnp.concatenate(parts + [fill], axis=0).astype(BF16)
        mine3 = (z - z_shift(l) + 8) % 8
        for o in range(1, 8):
            c3[l, o] = remote(
                s3[l].at[(mine3 + o) % 8], r3[l].at[z], s3_s.at[l, o], s3_r.at[l, o], pz(o))
        r3[l][z] = s3[l][mine3]

    finals = []

    def stage3(l):
        for o in range(1, 8):
            c3[l, o].wait_recv()
        tot = r3[l][0].astype(F32)
        for s in range(1, 8):
            tot = tot + r3[l][s].astype(F32)
        tot = jnp.concatenate([tot, jnp.zeros((8, 128), F32)], axis=0)
        for ct in range(3):
            fs[l][ct] = tot[UNIT * ct:UNIT * ct + 32].astype(BF16)
        for path in (1, 0):
            lo, hi = cols(l, path)
            tiles = pl.ds(lo // 128, (hi - lo) // 128)
            xx, tt, i = owner(l, path)
            own = jnp.logical_and(xx == x, tt == pos)
            src, dst = fs[l].at[tiles], fin_ref.at[i, tiles]
            far = pltpu.make_async_remote_copy(
                src_ref=src, dst_ref=dst, send_sem=fn_s.at[l, path], recv_sem=fn_r.at[i],
                device_id=dev(xx, tt), device_id_type=MESH)
            near = pltpu.make_async_copy(src, dst, fn_r.at[i])

            @pl.when(own)
            def _(near=near):
                near.start()

            @pl.when(jnp.logical_not(own))
            def _(far=far):
                far.start()
            finals.append((own, far))

    stage1(2, 1)
    stage1(2, 0)
    stage1(0, 1)
    stage1(0, 0)
    stage2(2)
    stage1(1, 1)
    stage1(1, 0)
    stage2(0)
    stage3(2)
    stage2(1)
    latent_out()
    stage3(0)
    stage3(1)

    for i in range(3):
        pltpu.make_async_copy(fin_ref.at[i], fin_ref.at[i], fn_r.at[i]).wait()

    for cp in started:
        cp.wait_send()
    for own, far in finals:
        @pl.when(jnp.logical_not(own))
        def _(far=far):
            far.wait_send()

    @pl.when(pos > 0)
    def _():
        for l in range(LAYERS):
            chain[l].wait_send()
    out_copy.wait()


def finish(lat_ref, unit_ref, latout_ref, wg_ref):
    latout_ref[...] = lat_ref[...]
    for ct in range(3):
        part = jnp.concatenate([unit_ref[i, ct].astype(F32)[0:UNIT] for i in range(3)], axis=0)
        wg_ref[:, 0, 128 * ct:128 * ct + 128] = part


def body(latents, caches, reward_grad, weights, biases, selected, destination):
    vmem = pltpu.VMEM
    per = lambda shape, kind: [vmem(shape(width(l, path)), kind) for l in range(LAYERS) for path in range(2)]
    scratch = [
        vmem((LAYERS, TAPS, CH, CH), BF16),
        vmem((LAYERS, 6, SPOTS, CH), BF16),
        vmem((FRAMES, SPOTS, CH), BF16),
        vmem((LAYERS, ROWS, CH), F32),
        vmem((ROWS, CH), F32),
        vmem((8, SPOTS, CH), BF16),
        vmem((LAYERS, 192, CH), BF16),
        vmem((LAYERS, 192, CH), BF16),
        vmem((FRAMES, SPOTS, CH), BF16),
    ]
    slices = [vmem((8, SL + 16 * (l == TOP), width(l, path)), BF16) for l in range(LAYERS) for path in range(2)]
    scratch += slices + slices
    scratch += per(lambda w: (4, SL, w), BF16)
    scratch += per(lambda w: (4, SL, w), BF16)
    scratch += [vmem((8, 64, 128), BF16)] * (2 * LAYERS)
    scratch += [vmem((3, 32, 128), BF16)] * LAYERS
    scratch += [vmem((2, 8, 8, 128), F32)]
    scratch += [vmem((LAYERS, CH), F32), vmem((1, 32), jnp.int32), vmem((1, 1), jnp.int32)]
    dma = pltpu.SemaphoreType.DMA
    scratch += [dma((11,)), dma((3,)), dma((3,))]
    scratch += [dma((3, 2, 8)), dma((3, 2, 8)), dma((3, 2, 4)), dma((3, 2, 4)), dma((3, 8)), dma((3, 8))]
    scratch += [dma((3, 2)), dma((3,)), dma(())]
    hbm = pl.BlockSpec(memory_space=pl.ANY)
    near = pl.BlockSpec(memory_space=pltpu.VMEM)
    latent_grad, units = pl.pallas_call(
        kernel,
        out_shape=(
            jax.ShapeDtypeStruct((1, FRAMES, SPOTS, CH), BF16),
            jax.ShapeDtypeStruct((3, 3, 32, 128), BF16),
        ),
        in_specs=[hbm] * 7,
        out_specs=(hbm, hbm),
        scratch_shapes=scratch,
        compiler_params=pltpu.CompilerParams(
            collective_id=0, has_side_effects=True, vmem_limit_bytes=63 * 1024 * 1024),
        cost_estimate=pl.CostEstimate(flops=3_060_000_000, bytes_accessed=5_000_000, transcendentals=450_000),
    )(latents, caches, reward_grad, weights, biases, selected, destination)
    latent_grad, block = pl.pallas_call(
        finish,
        out_shape=(
            jax.ShapeDtypeStruct((1, FRAMES, SPOTS, CH), BF16),
            jax.ShapeDtypeStruct((3 * UNIT, 1, CH), F32),
        ),
        in_specs=[near, near],
        out_specs=(near, near),
    )(latent_grad, units)
    return latent_grad, jnp.transpose(block, (1, 0, 2))


def solution(mesh):
    in_specs = (
        P("clip", "task", None, None),
        P("clip", "task", None, None, None, None),
        P("clip", "task", None, None),
        P(),
        P(),
        P("clip", None),
        P("clip", "task"),
    )
    out_specs = (P("clip", "task", None, None), P("clip", "task", None))
    return jax.shard_map(body, mesh=mesh, in_specs=in_specs, out_specs=out_specs, check_vma=False)
```

```python
import jax
import jax.numpy as jnp
from jax import lax
from jax.experimental import pallas as pl
from jax.experimental.pallas import tpu as pltpu
from jax.sharding import PartitionSpec as P

MESH = pl.DeviceIdType.MESH
F32 = jnp.float32
BF16 = jnp.bfloat16

CH = 384
FRAMES = 4
TAPS = 3
LAYERS = 3
SPOTS = 96
ROWS = FRAMES * SPOTS
NX, NY, NZ = 4, 4, 8
KR = TAPS * CH
SL = KR // 8
UNIT = SL // 8
TOP = LAYERS - 1
WIDTH_B = (256, 128, 256)


def cols(layer, path):
    wb = WIDTH_B[layer]
    return (wb, CH) if path == 0 else (0, wb)


def width(layer, path):
    lo, hi = cols(layer, path)
    return hi - lo


def task_of(y, z, c):
    return y * 16 + z * 2 + c


def kernel(*refs):
    it = iter(refs)
    take = lambda n: [next(it) for _ in range(n)]
    lat_hbm, cache_hbm, rg_hbm, w_hbm, bias_hbm, sel_hbm, dest_hbm = take(7)
    latout_hbm, fin_ref = take(2)
    w_ref, e_ref, rg_ref, sp_ref, g_ref, dpad_ref, leave_ref, in_ref, latg_ref = take(9)
    gbuf = [take(2) for _ in range(LAYERS)]
    r1 = [take(2) for _ in range(LAYERS)]
    s2 = [take(2) for _ in range(LAYERS)]
    r2 = [take(2) for _ in range(LAYERS)]
    s3 = take(LAYERS)
    r3 = take(LAYERS)
    fs = take(LAYERS)
    (mask_ref, bias_ref, sel_ref, dest_ref) = take(4)
    (ld_sem, ch_s, ch_r, s1_s, s1_r, s2_s, s2_r, s3_s, s3_r, fn_s, fn_r, out_sem) = take(12)

    x = lax.axis_index("clip")
    pos = lax.axis_index("task")
    y = pos // 16
    z = (pos % 16) // 2
    c = pos % 2

    loads = {}
    def load(name, src, dst, k):
        loads[name] = pltpu.make_async_copy(src, dst, ld_sem.at[k])
        loads[name].start()
    load("sel", sel_hbm, sel_ref, 8)
    load("dest", dest_hbm, dest_ref, 9)
    load("bias", bias_hbm, bias_ref, 10)
    load("lat", lat_hbm.at[0], e_ref.at[0, pl.ds(2, 4)], 0)
    for l in range(LAYERS):
        load(("c", l), cache_hbm.at[0, 0, l], e_ref.at[l, pl.ds(0, 2)], 1 + l)
        load(("w", l), w_hbm.at[l], w_ref.at[l], 4 + l)
    load("rg", rg_hbm.at[0], rg_ref, 7)

    def dev(xx, tt):
        return {"clip": xx, "task": tt}

    def b1(o):
        s = (2 * y + c + o) % 8
        return dev(x, task_of(s // 2, z, s % 2))

    def a1(o):
        s = (2 * x + c + o) % 8
        return dev(s // 2, task_of(y, z, s % 2))

    def px(o):
        return dev((x + o) % 4, pos)

    def py(o):
        return dev(x, task_of((y + o) % 4, z, c))

    def pz(o):
        return dev(x, task_of(y, (z + o) % 8, c))

    place1 = [2 * x + c, 2 * y + c]
    replica = [y, x]

    def z_shift(l):
        return 2 + 2 * l + l // 2

    def owner(l, path):
        u = 64 * l + 8 * ((z - z_shift(l) + 8) % 8) + place1[path]
        return replica[path], u // 3, u % 3

    def source(i, path):
        u = 3 * pos + i
        l, m, s = u // 64, (u % 64) // 8, u % 8
        zz = (m + z_shift(l)) % 8
        if path == 1:
            return dev(x, task_of(s // 2, zz, s % 2))
        return dev(s // 2, task_of(x, zz, s % 2))

    barrier = pltpu.get_barrier_semaphore()
    greet = [b1(o) for o in range(1, 8)] + [a1(o) for o in range(1, 8)]
    greet += [px(o) for o in range(1, 4)] + [py(o) for o in range(1, 4)] + [pz(o) for o in range(1, 8)]
    greet += [dev(x, (pos + 1) % 64)]
    greet += [source(i, path) for i in range(3) for path in range(2)]
    for who in greet:
        pl.semaphore_signal(barrier, inc=1, device_id=who, device_id_type=MESH)

    for name in ("sel", "dest", "bias"):
        loads[name].wait()
    flag = jnp.max((sel_ref[...] == pos).astype(F32), axis=1, keepdims=True)
    for path in range(2):
        w = width(TOP, path)
        mask = (lax.broadcasted_iota(jnp.int32, (16, w), 0) == dest_ref[...]).astype(F32).astype(BF16)
        for s in range(8):
            gbuf[TOP][path][s, SL:SL + 16] = mask
    dpad_ref[pl.ds(0, 2)] = jnp.zeros((2, SPOTS, CH), BF16)
    dpad_ref[pl.ds(6, 2)] = jnp.zeros((2, SPOTS, CH), BF16)

    @pl.when(pos == 63)
    def _():
        in_ref[...] = jnp.zeros(in_ref.shape, BF16)

    loads["lat"].wait()
    for l in range(LAYERS):
        loads[("c", l)].wait()
        loads[("w", l)].wait()
        lhs = jnp.concatenate([e_ref[l, k:k + 4].reshape(ROWS, CH) for k in range(TAPS)], axis=1)
        a = jnp.dot(lhs, w_ref[l].reshape(KR, CH), preferred_element_type=F32) + bias_ref[l:l + 1, :]
        sg = jax.nn.sigmoid(a)
        sp_ref[l] = sg * (1.0 + a * (1.0 - sg))
        if l < LAYERS - 1:
            h = e_ref[l, 2:6].reshape(ROWS, CH).astype(F32) + a * sg
            e_ref[l + 1, 2:6] = h.astype(BF16).reshape(FRAMES, SPOTS, CH)

    pl.semaphore_wait(barrier, len(greet))
    started = []

    def remote(src, dst, ssem, rsem, who):
        cp = pltpu.make_async_remote_copy(
            src_ref=src, dst_ref=dst, send_sem=ssem, recv_sem=rsem, device_id=who, device_id_type=MESH)
        cp.start()
        started.append(cp)
        return cp

    loads["rg"].wait()
    g_ref[...] = rg_ref[...].reshape(ROWS, CH).astype(F32) * flag

    mine = place1
    first = [a1, b1]
    c1 = {}
    chain = {}
    def send1(l, path):
        for o in (4, 3, 5, 2, 6, 1, 7):
            s = (mine[path] + o) % 8
            c1[l, path, o] = remote(
                gbuf[l][path].at[s], r1[l][path].at[mine[path]],
                s1_s.at[l, path, o], s1_r.at[l, path, o], first[path](o))
        r1[l][path][mine[path]] = gbuf[l][path][mine[path]]

    for l in range(LAYERS - 1, -1, -1):
        if l < LAYERS - 1:
            @pl.when(pos < 63)
            def _(l=l):
                chain[l + 1].wait_recv()
            g_ref[pl.ds(192, 192)] += in_ref[l + 1].astype(F32)
        d = (g_ref[...] * sp_ref[l]).astype(BF16)
        dpad_ref[pl.ds(2, 4)] = d.reshape(FRAMES, SPOTS, CH)
        def lead_out(l=l, d=d):
            lhs = jnp.concatenate([dpad_ref[2:4].reshape(192, CH), dpad_ref[1:3].reshape(192, CH)], axis=1)
            rhs = jnp.concatenate([w_ref[l, 0], w_ref[l, 1]], axis=1)
            lead = lax.dot_general(lhs, rhs, (((1,), (1,)), ((), ())), preferred_element_type=F32)
            leave_ref[l] = lead.astype(BF16)
            chain[l] = pltpu.make_async_remote_copy(
                src_ref=leave_ref.at[l], dst_ref=in_ref.at[l], send_sem=ch_s.at[l], recv_sem=ch_r.at[l],
                device_id=dev(x, (pos + 63) % 64), device_id_type=MESH)

            @pl.when(pos > 0)
            def _(l=l):
                chain[l].start()

        def kernel_grad(l=l):
            pad = jnp.zeros((32, CH), BF16)
            et = jnp.concatenate([v for f in range(6) for v in (e_ref[l, f], pad)], axis=0).T
            et = jnp.concatenate([et[:, 128 * k:128 * k + 512] for k in range(TAPS)], axis=0)
            dp = jnp.concatenate([v for f in range(FRAMES) for v in (dpad_ref[2 + f], pad)], axis=0)
            for path in (1, 0):
                lo, hi = cols(l, path)
                grads = jnp.dot(et, dp[:, lo:hi], preferred_element_type=F32)
                for s in range(8):
                    rows = [grads[SL * m + UNIT * s:SL * m + UNIT * s + UNIT] for m in range(8)]
                    gbuf[l][path][s, 0:SL] = jnp.concatenate(rows, axis=0).astype(BF16)
                if l != 1:
                    send1(l, path)
        if l == LAYERS - 1:
            kernel_grad()
            lead_out()
        else:
            lead_out()
            kernel_grad()
        if l == 0:
            send1(1, 1)
            send1(1, 0)

        lhs = jnp.concatenate([dpad_ref[4 - k:8 - k].reshape(ROWS, CH) for k in range(TAPS)], axis=1)
        rhs = jnp.concatenate([w_ref[l, k] for k in range(TAPS)], axis=1)
        g_ref[...] += lax.dot_general(lhs, rhs, (((1,), (1,)), ((), ())), preferred_element_type=F32)

    out_copy = pltpu.make_async_copy(latg_ref, latout_hbm.at[0], out_sem)

    def latent_out():
        @pl.when(pos < 63)
        def _():
            chain[0].wait_recv()
        g_ref[pl.ds(192, 192)] += in_ref[0].astype(F32)
        latg_ref[...] = g_ref[...].astype(BF16).reshape(FRAMES, SPOTS, CH)
        out_copy.start()

    second = [py, px]
    here = [y, x]
    c2, c3 = {}, {}

    def stage1(l, path):
        w = width(l, path)
        for o in range(1, 8):
            c1[l, path, o].wait_recv()
        if l == TOP:
            for s in range(8):
                mask_ref[path, s] = r1[l][path][s, SL:SL + 16, 0:128].astype(F32)[0:8]

        def step(i, _):
            rows = pl.ds(pl.multiple_of(i * 16, 16), 16)
            for lane in range(0, w, 128):
                at = slice(lane, lane + 128)
                raw = [r1[l][path][s, rows, at].astype(F32) for s in range(8)]
                for r in range(4):
                    tot = raw[0] * mask_ref[path, 0, r:r + 1, :]
                    for s in range(1, 8):
                        tot = tot + raw[s] * mask_ref[path, s, r:r + 1, :]
                    s2[l][path][r, rows, at] = tot.astype(BF16)
            return 0

        lax.fori_loop(0, SL // 16, step, 0)
        for o in (2, 1, 3):
            c2[l, path, o] = remote(
                s2[l][path].at[(here[path] + o) % 4], r2[l][path].at[here[path]],
                s2_s.at[l, path, o], s2_r.at[l, path, o], second[path](o))
        r2[l][path][here[path]] = s2[l][path][here[path]]

    def stage2(l):
        tiles = [None] * 3
        for path in (1, 0):
            lo, hi = cols(l, path)
            for o in range(1, 4):
                c2[l, path, o].wait_recv()
            tot = r2[l][path][0].astype(F32)
            for s in range(1, 4):
                tot = tot + r2[l][path][s].astype(F32)
            for lane in range(lo, hi, 128):
                tiles[lane // 128] = tot[:, lane - lo:lane - lo + 128]
        fill = jnp.zeros((10, 128), F32)
        for m in range(8):
            parts = [t[UNIT * m:UNIT * m + UNIT] for t in tiles]
            s3[l][m] = jnp.concatenate(parts + [fill], axis=0).astype(BF16)
        mine3 = (z - z_shift(l) + 8) % 8
        for o in (4, 3, 5, 2, 6, 1, 7):
            c3[l, o] = remote(
                s3[l].at[(mine3 + o) % 8], r3[l].at[z], s3_s.at[l, o], s3_r.at[l, o], pz(o))
        r3[l][z] = s3[l][mine3]

    finals = []

    def stage3(l):
        for o in range(1, 8):
            c3[l, o].wait_recv()
        tot = r3[l][0].astype(F32)
        for s in range(1, 8):
            tot = tot + r3[l][s].astype(F32)
        tot = jnp.concatenate([tot, jnp.zeros((8, 128), F32)], axis=0)
        for ct in range(3):
            fs[l][ct] = tot[UNIT * ct:UNIT * ct + 32].astype(BF16)
        for path in (1, 0):
            lo, hi = cols(l, path)
            tiles = pl.ds(lo // 128, (hi - lo) // 128)
            xx, tt, i = owner(l, path)
            own = jnp.logical_and(xx == x, tt == pos)
            src, dst = fs[l].at[tiles], fin_ref.at[i, tiles]
            far = pltpu.make_async_remote_copy(
                src_ref=src, dst_ref=dst, send_sem=fn_s.at[l, path], recv_sem=fn_r.at[i],
                device_id=dev(xx, tt), device_id_type=MESH)
            near = pltpu.make_async_copy(src, dst, fn_r.at[i])

            @pl.when(own)
            def _(near=near):
                near.start()

            @pl.when(jnp.logical_not(own))
            def _(far=far):
                far.start()
            finals.append((own, far))

    stage1(2, 1)
    stage1(2, 0)
    stage1(0, 1)
    stage1(0, 0)
    stage2(2)
    stage1(1, 1)
    stage1(1, 0)
    stage2(0)
    stage2(1)
    stage3(2)
    stage3(0)
    stage3(1)
    latent_out()

    for i in range(3):
        pltpu.make_async_copy(fin_ref.at[i], fin_ref.at[i], fn_r.at[i]).wait()

    for cp in started:
        cp.wait_send()
    for own, far in finals:
        @pl.when(jnp.logical_not(own))
        def _(far=far):
            far.wait_send()

    @pl.when(pos > 0)
    def _():
        for l in range(LAYERS):
            chain[l].wait_send()
    out_copy.wait()


def finish(lat_ref, units_ref, latout_ref, wgout_ref, lat, unit_ref, wg_ref, sem_in, sem_out):
    into = [pltpu.make_async_copy(units_ref, unit_ref, sem_in.at[FRAMES])]
    into += [pltpu.make_async_copy(lat_ref.at[0, f], lat.at[f], sem_in.at[f]) for f in range(FRAMES)]
    out = [pltpu.make_async_copy(lat.at[f], latout_ref.at[0, f], sem_out.at[f]) for f in range(FRAMES)]
    out += [pltpu.make_async_copy(wg_ref, wgout_ref, sem_out.at[FRAMES])]
    for copy in into:
        copy.start()
    into[0].wait()
    for ct in range(3):
        part = jnp.concatenate([unit_ref[i, ct].astype(F32)[0:UNIT] for i in range(3)], axis=0)
        wg_ref[:, 0, 128 * ct:128 * ct + 128] = part
    out[FRAMES].start()
    for f in range(FRAMES):
        into[1 + f].wait()
        out[f].start()
    for copy in out:
        copy.wait()


def body(latents, caches, reward_grad, weights, biases, selected, destination):
    vmem = pltpu.VMEM
    per = lambda shape, kind: [vmem(shape(width(l, path)), kind) for l in range(LAYERS) for path in range(2)]
    scratch = [
        vmem((LAYERS, TAPS, CH, CH), BF16),
        vmem((LAYERS, 6, SPOTS, CH), BF16),
        vmem((FRAMES, SPOTS, CH), BF16),
        vmem((LAYERS, ROWS, CH), F32),
        vmem((ROWS, CH), F32),
        vmem((8, SPOTS, CH), BF16),
        vmem((LAYERS, 192, CH), BF16),
        vmem((LAYERS, 192, CH), BF16),
        vmem((FRAMES, SPOTS, CH), BF16),
    ]
    slices = [vmem((8, SL + 16 * (l == TOP), width(l, path)), BF16) for l in range(LAYERS) for path in range(2)]
    scratch += slices + slices
    scratch += per(lambda w: (4, SL, w), BF16)
    scratch += per(lambda w: (4, SL, w), BF16)
    scratch += [vmem((8, 64, 128), BF16)] * (2 * LAYERS)
    scratch += [vmem((3, 32, 128), BF16)] * LAYERS
    scratch += [vmem((2, 8, 8, 128), F32)]
    scratch += [vmem((LAYERS, CH), F32), vmem((1, 32), jnp.int32), vmem((1, 1), jnp.int32)]
    dma = pltpu.SemaphoreType.DMA
    scratch += [dma((11,)), dma((3,)), dma((3,))]
    scratch += [dma((3, 2, 8)), dma((3, 2, 8)), dma((3, 2, 4)), dma((3, 2, 4)), dma((3, 8)), dma((3, 8))]
    scratch += [dma((3, 2)), dma((3,)), dma(())]
    hbm = pl.BlockSpec(memory_space=pl.ANY)
    latent_grad, units = pl.pallas_call(
        kernel,
        out_shape=(
            jax.ShapeDtypeStruct((1, FRAMES, SPOTS, CH), BF16),
            jax.ShapeDtypeStruct((3, 3, 32, 128), BF16),
        ),
        in_specs=[hbm] * 7,
        out_specs=(hbm, hbm),
        scratch_shapes=scratch,
        compiler_params=pltpu.CompilerParams(
            collective_id=0, has_side_effects=True, vmem_limit_bytes=63 * 1024 * 1024),
        cost_estimate=pl.CostEstimate(flops=3_060_000_000, bytes_accessed=5_000_000, transcendentals=450_000),
    )(latents, caches, reward_grad, weights, biases, selected, destination)
    latent_grad, block = pl.pallas_call(
        finish,
        out_shape=(
            jax.ShapeDtypeStruct((1, FRAMES, SPOTS, CH), BF16),
            jax.ShapeDtypeStruct((3 * UNIT, 1, CH), F32),
        ),
        in_specs=[hbm, hbm],
        out_specs=(hbm, hbm),
        scratch_shapes=[
            vmem((FRAMES, SPOTS, CH), BF16),
            vmem((3, 3, 32, 128), BF16),
            vmem((3 * UNIT, 1, CH), F32),
            pltpu.SemaphoreType.DMA((FRAMES + 1,)),
            pltpu.SemaphoreType.DMA((FRAMES + 1,)),
        ],
    )(latent_grad, units)
    return latent_grad, jnp.transpose(block, (1, 0, 2))


def solution(mesh):
    in_specs = (
        P("clip", "task", None, None),
        P("clip", "task", None, None, None, None),
        P("clip", "task", None, None),
        P(),
        P(),
        P("clip", None),
        P("clip", "task"),
    )
    out_specs = (P("clip", "task", None, None), P("clip", "task", None))
    return jax.shard_map(body, mesh=mesh, in_specs=in_specs, out_specs=out_specs, check_vma=False)
```
